32 devices in a mesh: expert: 8 (over y, x, core), tensor: 4 (over z).
Axes of the slice: x: 2, y: 2, z: 4, core: 2. Of those that a mesh axis runs over, the one named last changes fastest.
Arguments:
- tokens: bfloat16 [1024, 7168], P('expert', 'tensor'), may hold values from -6 to 6
- grad_out: bfloat16 [1024, 7168], P('expert', 'tensor'), may hold values from -6 to 6
- expert_ids: int32 [1024, 2], P('expert'), may hold values from 0 to 7, all different within a row; in each aligned block of 128 rows (0 to 127, 128 to 255, ...) at most 64 rows name the same one
- gates: float32 [1024, 2], P('expert'), may hold values from 0.1 to 1
- w_gate: bfloat16 [8, 7168, 2048], P('expert', None, 'tensor'), may hold values from -0.0625 to 0.0625
- w_up: bfloat16 [8, 7168, 2048], P('expert', None, 'tensor'), may hold values from -0.0625 to 0.0625
- w_down: bfloat16 [8, 2048, 7168], P('expert', 'tensor'), may hold values from -0.125 to 0.125
Outputs:
- grad_tokens: bfloat16 [1024, 7168], P('expert', 'tensor')
- grad_w_gate: bfloat16 [8, 7168, 2048], P('expert', None, 'tensor')
- grad_w_up: bfloat16 [8, 7168, 2048], P('expert', None, 'tensor')
- grad_w_down: bfloat16 [8, 2048, 7168], P('expert', 'tensor')
The draws below stay inside these ranges and needn't reach their ends.
Inputs may be any that keep to these rules, and one draw needn't show every extreme that they name: `expert_ids`: each token names 2 different experts. In each aligned block of 128 tokens (the tokens of one index of the expert axis), no expert is named by more than 64 routes, a bound that some block reaches.
All inputs are finite; a program needn't handle non-finite values.
Results may differ from the reference program's by a relative error of at most 0.0057.
Values may be sent and summed in bfloat16 or wider, within the bound.
No kernel may reach another device: no remote copies, remote signals or barrier semaphores. Data moves between devices by JAX's collectives and lax.ppermute only.
A program may use at most 192 MiB of HBM per device.

```python
import math
import jax
import jax.numpy as jnp
import numpy as np
from jax import lax

D = 7168
FF = 2048
TOK_DEV = 128
TOP = 2
EXPERTS = 8
CAP = 64
TOKENS = 1024
N_EXPERT = 8


def steps_of(stream_key, dims, shards, least, top_value):
    level, own = 1.0, jax.random.fold_in(stream_key, 6)
    for axis_at, shards_of in shards:
        heights = jnp.exp(jax.random.uniform(jax.random.fold_in(own, axis_at), (shards_of,), jnp.float32, least / len(shards), top_value / len(shards)))
        level = level * jnp.repeat(heights, dims[axis_at] // shards_of).reshape([-1 if axis == axis_at else 1 for axis in range(len(dims))])
    return level


def assign_block(key, own, number, rows, number_of, top, limit, slope):
    ranking = jax.random.permutation(key, number_of)
    crowded, usual = portions_of(number_of, rows * top, limit, slope, True), portions_of(number_of, rows * top, limit, slope, False)
    places = jnp.arange(number_of)

    def named(tallies, turn):
        used = int((tallies > 0).sum())
        fixed = max(1, used // 4)
        moved = fixed + (places - fixed + turn * (used - fixed)) % max(1, number_of - fixed)
        return jnp.zeros((number_of,), jnp.int32).at[ranking[jnp.where(places < fixed, places, moved)]].set(jnp.asarray(tallies, jnp.int32))

    tallies = jnp.where(number % 4 == 0, named(crowded, number // 4), named(usual, number - number // 4 - 1))
    mixed = jax.random.permutation(jax.random.fold_in(own, 3), number_of)
    source_of, receiver = mixed[0:number_of // 2 * 2:2], mixed[1:number_of // 2 * 2:2]
    slack = jnp.minimum(tallies[source_of] - 1, limit - tallies[receiver]) // 2
    slack = jnp.where((source_of == ranking[0]) | (receiver == ranking[0]) | (tallies[receiver] == 0), 0, jnp.maximum(slack, 0))
    moved = jax.random.randint(jax.random.fold_in(own, 4), (number_of // 2,), 0, 1 << 20) % (slack + 1)
    tallies = tallies.at[source_of].add(-moved).at[receiver].add(moved)
    items = jnp.searchsorted(jnp.cumsum(tallies), jnp.arange(rows * top), side="right").astype(jnp.int32)
    grid = items.reshape(top, rows).T
    grid = grid[jax.random.permutation(jax.random.fold_in(own, 1), rows)]
    turn = jax.random.randint(jax.random.fold_in(own, 2), (rows, 1), 0, top)
    return jnp.take_along_axis(grid, (jnp.arange(top)[None, :] + turn) % top, axis=1)


def portions_of(number_of, total, reach, slope, full):
    portions = [(1 << 20) // math.isqrt(standing ** slope) + 1 for standing in range(1, number_of + 1)]
    largest = reach if full else min(reach, max(-(-total // number_of), total * portions[0] // sum(portions)))
    least = 1 if total - largest >= number_of - 1 else 0
    given, rest = [largest] + [least] * (number_of - 1), total - largest - least * (number_of - 1)
    while rest > 0:
        candidates = [i for i in range(1, number_of) if given[i] < largest] or [i for i in range(1, number_of) if given[i] < reach]
        pool, remaining = sum([portions[i] for i in candidates]), rest
        for i in candidates:
            addition = min(reach - given[i], max(1, remaining * portions[i] // pool), rest)
            given[i] = given[i] + addition
            rest = rest - addition
    return np.array(given)


def centred(rng, shape, spread, reach, cuts=(), held_as=jnp.bfloat16):
    loudness = steps_of(rng, shape, cuts, -0.22, 0.18) if cuts else 1.0
    drawn = jax.random.normal(rng, shape, jnp.float32) * spread * loudness
    return jnp.minimum(jnp.maximum(drawn, -reach), reach).astype(held_as)


def setup_inputs(seed: int = 0) -> dict:
    streams_of = jax.random.split(jax.random.key(seed), 8)
    tokens = centred(streams_of[0], (TOKENS, D), 1.0, 6.0, ((0, 8), (1, 4)))
    grad_out = centred(streams_of[1], (TOKENS, D), 1.0, 6.0, ((0, 8), (1, 4)))
    expert_ids_keys = jax.random.split(jax.random.fold_in(streams_of[2], 1), TOKENS // TOK_DEV)
    expert_ids_turns = jax.random.permutation(jax.random.fold_in(streams_of[2], 3), TOKENS // TOK_DEV)
    expert_ids = jax.vmap(lambda own, number: assign_block(jax.random.fold_in(streams_of[2], 2), own, number, TOK_DEV, EXPERTS, TOP, CAP, 2))(expert_ids_keys, expert_ids_turns).reshape((TOKENS, TOP))
    gates = jnp.clip(jnp.exp(math.log(1.0) - 2.3025851 * jax.random.uniform(streams_of[3], (TOKENS, TOP), jnp.float32) ** steps_of(streams_of[3], (TOKENS, TOP), ((0, 8),), -0.2, 0.2)), 0.1, 1.0)
    w_gate = centred(streams_of[4], (EXPERTS, D, FF), D ** -0.5, 0.0625, ((0, 8), (2, 4)))
    w_up = centred(streams_of[5], (EXPERTS, D, FF), D ** -0.5, 0.0625, ((0, 8), (2, 4)))
    w_down = centred(streams_of[6], (EXPERTS, FF, D), FF ** -0.5, 0.125, ((0, 8), (1, 4)))
    return dict(tokens=tokens, grad_out=grad_out, expert_ids=expert_ids, gates=gates, w_gate=w_gate, w_up=w_up, w_down=w_down)


def route_slots(expert_ids):
    blocks = expert_ids.reshape(N_EXPERT, TOK_DEV * TOP)
    onehot = (blocks[:, :, None] == jnp.arange(EXPERTS, dtype=jnp.int32)[None, None, :]).astype(jnp.int32)
    before = jnp.cumsum(onehot, axis=1) - onehot
    slot = jnp.sum(before * onehot, axis=2)
    source = jnp.arange(N_EXPERT, dtype=jnp.int32)[:, None]
    return blocks.reshape(-1), (source * CAP + slot).reshape(-1).astype(jnp.int32)


def expert_backward(packed):
    rows_in, grads_in, wg, wu, wd = packed
    gate = jnp.dot(rows_in, wg, preferred_element_type=jnp.float32)
    upper = jnp.dot(rows_in, wu, preferred_element_type=jnp.float32)
    sig = jax.nn.sigmoid(gate)
    act = gate * sig
    hidden = (act * upper).astype(jnp.bfloat16)
    dhidden = jnp.dot(grads_in, wd.T, preferred_element_type=jnp.float32)
    dgate = (dhidden * upper * sig * (1.0 + gate * (1.0 - sig))).astype(jnp.bfloat16)
    dup = (dhidden * act).astype(jnp.bfloat16)
    dx_rows = jnp.dot(dgate, wg.T, preferred_element_type=jnp.float32) + jnp.dot(dup, wu.T, preferred_element_type=jnp.float32)
    dwg = jnp.dot(rows_in.T, dgate, preferred_element_type=jnp.float32).astype(jnp.bfloat16)
    dwu = jnp.dot(rows_in.T, dup, preferred_element_type=jnp.float32).astype(jnp.bfloat16)
    dwd = jnp.dot(hidden.T, grads_in, preferred_element_type=jnp.float32).astype(jnp.bfloat16)
    return dx_rows, dwg, dwu, dwd


def reference(tokens, grad_out, expert_ids, gates, w_gate, w_up, w_down):
    target, position = route_slots(expert_ids)
    weighted = (gates[:, :, None] * grad_out[:, None, :].astype(jnp.float32)).astype(jnp.bfloat16)
    weighted = weighted.reshape(TOKENS * TOP, D)
    repeated = jnp.repeat(tokens, TOP, axis=0)
    empty = jnp.zeros((EXPERTS, N_EXPERT * CAP, D), jnp.bfloat16)
    rows_in = empty.at[target, position].set(repeated)
    grads_in = empty.at[target, position].set(weighted)
    dx_rows, dwg, dwu, dwd = lax.map(expert_backward, (rows_in, grads_in, w_gate, w_up, w_down))
    picked = dx_rows[target, position]
    grad_tokens = jnp.sum(picked.reshape(TOKENS, TOP, D), axis=1).astype(jnp.bfloat16)
    return grad_tokens, dwg, dwu, dwd
```

```python
import functools

import jax
import jax.numpy as jnp
from jax import lax
from jax.sharding import PartitionSpec as P

BF16 = jnp.bfloat16
F32 = jnp.float32


def swap(a, mask):
    n = lax.axis_size("expert")
    return lax.ppermute(a, "expert", [(i, i ^ mask) for i in range(n)])


def ring(a):
    n = lax.axis_size("tensor")
    return lax.ppermute(a, "tensor", [(i, (i + 1) % n) for i in range(n)])


def far_masks():
    n = lax.axis_size("expert")
    return [1 << b for b in range(1, n.bit_length() - 1)]


def block_order():
    n = lax.axis_size("expert")
    near = [0]
    for m in far_masks():
        near = near + [k ^ m for k in near]
    return near + [k ^ 1 for k in near]


def gather_rows(own):
    far = far_masks()
    if len(far) == 2:
        h = own.shape[0] // 2
        x = swap(own, far[0])
        y = swap(own, far[1])
        da = swap(x[:h], far[1])
        db = swap(y[h:], far[0])
        pieces = [own, x, y, da, db]
    else:
        pieces = [own]
        for m in far:
            pieces = pieces + [swap(p, m) for p in pieces]
    return pieces + [swap(p, 1) for p in pieces]


def scatter_rows(part, rows):
    half = part.shape[0] // 2
    far = far_masks()
    got = swap(part[half:], 1)
    mine = part[:half].astype(F32) + got.astype(F32)
    mine = mine.astype(BF16).reshape(half // rows, rows, -1)
    if len(far) == 2:
        h = rows // 2
        ex = swap(mine[3, :h], far[0])
        ey = swap(mine[3, h:], far[1])
        fx_a = swap(mine[1, :h], far[0])
        fy_b = swap(mine[2, h:], far[1])
        fy_a = swap((mine[2, :h].astype(F32) + ex.astype(F32)).astype(BF16), far[1])
        fx_b = swap((mine[1, h:].astype(F32) + ey.astype(F32)).astype(BF16), far[0])
        return [
            mine[0],
            jnp.concatenate([fx_a, fx_b]),
            jnp.concatenate([fy_a, fy_b]),
        ]
    for m in reversed(far):
        cut = mine.shape[0] // 2
        got = swap(mine[cut:], m)
        mine = (mine[:cut].astype(F32) + got.astype(F32)).astype(BF16)
    return [mine[0]]


def total(terms):
    return functools.reduce(lambda a, b: a + b, [t.astype(F32) for t in terms])


def on_device(tokens, grad_out, expert_ids, gates, w_gate, w_up, w_down):
    owners, shards = lax.axis_size("expert"), lax.axis_size("tensor")
    me, z = lax.axis_index("expert"), lax.axis_index("tensor")
    rows, width = tokens.shape
    wg, wu, wd = w_gate[0], w_up[0], w_down[0]
    order = block_order()

    chosen = expert_ids[:, :, None] == jnp.arange(owners, dtype=jnp.int32)
    weights = jnp.sum(jnp.where(chosen, gates[:, :, None], 0.0), axis=1)
    weights = lax.all_to_all(weights.T, "expert", split_axis=0, concat_axis=0, tiled=True)
    weights = weights[me ^ jnp.array(order, dtype=jnp.int32)].reshape(-1, 1)

    at = [lax.rem(z - j + shards, shards) * width for j in range(shards)]
    cut_rows = lambda w, j: lax.dynamic_slice_in_dim(w, at[j], width, 0)
    cut_cols = lambda w, j: lax.dynamic_slice_in_dim(w, at[j], width, 1)

    def gather(own):
        out = []
        for j in range(shards):
            if j:
                own = ring(own)
            out.append(gather_rows(own))
        return out

    x = [jnp.concatenate(p) for p in gather(tokens)]
    gate = total([jnp.dot(x[j], cut_rows(wg, j), preferred_element_type=F32) for j in range(shards)])
    upper = total([jnp.dot(x[j], cut_rows(wu, j), preferred_element_type=F32) for j in range(shards)])
    g = [(weights * jnp.concatenate(p).astype(F32)).astype(BF16) for p in gather(grad_out)]
    last = (((1,), (1,)), ((), ()))
    first = (((0,), (0,)), ((), ()))
    dot = functools.partial(lax.dot_general, preferred_element_type=F32)
    dhidden = total([dot(g[j], cut_cols(wd, j), last) for j in range(shards)])

    sig = jax.nn.sigmoid(gate)
    act = gate * sig
    hidden = (act * upper).astype(BF16)
    dgate = (dhidden * upper * sig * (1.0 + gate * (1.0 - sig))).astype(BF16)
    dup = (dhidden * act).astype(BF16)

    run = None
    for j in list(range(1, shards)) + [0]:
        part = dot(dgate, cut_rows(wg, j), last) + dot(dup, cut_rows(wu, j), last)
        terms = scatter_rows(part.astype(BF16), rows)
        if run is not None:
            terms.append(ring(run))
        run = total(terms).astype(BF16)

    grad_wg = jnp.zeros(wg.shape, BF16)
    grad_wu = jnp.zeros(wu.shape, BF16)
    grad_wd = jnp.zeros(wd.shape, BF16)
    for j in range(shards):
        grad_wg = lax.dynamic_update_slice_in_dim(grad_wg, dot(x[j], dgate, first).astype(BF16), at[j], 0)
        grad_wu = lax.dynamic_update_slice_in_dim(grad_wu, dot(x[j], dup, first).astype(BF16), at[j], 0)
        grad_wd = lax.dynamic_update_slice_in_dim(grad_wd, dot(hidden, g[j], first).astype(BF16), at[j], 1)
    return (run, grad_wg[None], grad_wu[None], grad_wd[None])


def solution(mesh):
    placed = (
        P("expert", "tensor"),
        P("expert", "tensor"),
        P("expert", None),
        P("expert", None),
        P("expert", None, "tensor"),
        P("expert", None, "tensor"),
        P("expert", "tensor", None),
    )
    return jax.shard_map(
        on_device,
        mesh=mesh,
        in_specs=placed,
        out_specs=(
            P("expert", "tensor"),
            P("expert", None, "tensor"),
            P("expert", None, "tensor"),
            P("expert", "tensor", None),
        ),
        check_vma=False,
    )
```

```python
import functools

import jax
import jax.numpy as jnp
from jax import lax
from jax.experimental import pallas as pl
from jax.experimental.pallas import tpu as pltpu
from jax.sharding import PartitionSpec as P

BF16 = jnp.bfloat16
F32 = jnp.float32
LAST = (((1,), (1,)), ((), ()))
FIRST = (((0,), (0,)), ((), ()))
PLAIN = (((1,), (0,)), ((), ()))

dot = functools.partial(lax.dot_general, preferred_element_type=F32)


def after(a, *others):
    return lax.optimization_barrier((a,) + others)[0]


def swap(a, mask):
    n = lax.axis_size("expert")
    return lax.ppermute(a, "expert", [(i, i ^ mask) for i in range(n)])


def ring(a):
    n = lax.axis_size("tensor")
    return lax.ppermute(a, "tensor", [(i, (i + 1) % n) for i in range(n)])


class Links:
    def __init__(self):
        self.held, self.now = [], []

    def turn(self, *work):
        self.held, self.now = self.now + list(work), []

    def send(self, link, a):
        if self.held:
            a = after(a, *self.held)
        self.now.append(ring(a) if link == 0 else swap(a, link))
        return self.now[-1]


def far_masks():
    n = lax.axis_size("expert")
    return [1 << b for b in range(1, n.bit_length() - 1)]


def stack(refs, places, rows):
    return jnp.concatenate([refs[i][at : at + rows, :] for i, at in places], axis=0)


def chunk_of(width, most):
    return max(c for c in range(128, most + 1, 128) if width % c == 0)


def spec(shape, index):
    return pl.BlockSpec(shape, index)


def fixed(a):
    return pl.BlockSpec(a.shape, lambda k, s: (0,) * a.ndim)


def call(kernel, name, at, grid, ins, in_specs, outs, out_specs, scratch=(), aliases=None, flops=0):
    moved = sum(a.size * a.dtype.itemsize for a in ins) + sum(
        o.size * o.dtype.itemsize for o in outs
    )
    return pl.pallas_call(
        kernel,
        out_shape=outs,
        grid_spec=pltpu.PrefetchScalarGridSpec(
            num_scalar_prefetch=1,
            grid=(grid,),
            in_specs=in_specs,
            out_specs=out_specs,
            scratch_shapes=list(scratch),
        ),
        input_output_aliases=aliases or {},
        compiler_params=pltpu.CompilerParams(
            dimension_semantics=("arbitrary",), vmem_limit_bytes=48 * 2**20
        ),
        cost_estimate=pl.CostEstimate(flops=flops, bytes_accessed=moved, transcendentals=0),
        name=name,
    )(at, *ins)


def forward(at, parts, rows, weight, wg, wu, wd, sums, final):
    arrays, tok, grd = parts
    n, (width, ff), count = len(arrays), (arrays[0].shape[1], wg.shape[1]), len(tok) * rows
    ck = chunk_of(width, 896)
    steps = width // ck

    def kernel(_, *refs):
        xs, (w_ref, g_ref, u_ref, d_ref) = refs[:n], refs[n : n + 4]
        rest = refs[n + 4 :]
        before = rest[: len(sums)]
        outs = rest[len(sums) :]
        accs = outs[3:] if final else outs
        k = pl.program_id(0)

        @pl.when(k == 0)
        def _():
            for i, acc in enumerate(accs):
                acc[...] = before[i][...] if sums else jnp.zeros_like(acc)

        x = stack(xs, tok, rows)
        accs[0][...] += dot(x, g_ref[...], PLAIN)
        accs[1][...] += dot(x, u_ref[...], PLAIN)
        g = (w_ref[...] * stack(xs, grd, rows).astype(F32)).astype(BF16)
        accs[2][...] += dot(g, d_ref[...], LAST)
        if final:

            @pl.when(k == steps - 1)
            def _():
                def piece(i, _):
                    at = pl.ds(pl.multiple_of(i * rows, rows), rows)
                    gate, upper, dh = accs[0][at, :], accs[1][at, :], accs[2][at, :]
                    sig = jax.nn.sigmoid(gate)
                    act = gate * sig
                    outs[0][at, :] = (act * upper).astype(BF16)
                    outs[1][at, :] = (dh * upper * sig * (1.0 + gate * (1.0 - sig))).astype(BF16)
                    outs[2][at, :] = (dh * act).astype(BF16)
                    return _

                lax.fori_loop(0, count // rows, piece, 0)

    out = jax.ShapeDtypeStruct((count, ff), BF16 if final else F32)
    in_specs = [spec((a.shape[0], ck), lambda k, s: (0, k)) for a in arrays] + [
        fixed(weight),
        spec((ck, ff), lambda k, s: (s[0] * steps + k, 0)),
        spec((ck, ff), lambda k, s: (s[0] * steps + k, 0)),
        spec((ff, ck), lambda k, s: (0, s[0] * steps + k)),
    ]
    in_specs += [fixed(a) for a in sums]
    return call(
        kernel, "forward", at, steps, [*arrays, weight, wg, wu, wd, *sums], in_specs,
        [out] * 3, [fixed(out)] * 3,
        scratch=[pltpu.VMEM((count, ff), F32)] * 3 if final else (),
        flops=6 * count * width * ff,
    )


def inputs_back(at, dgate, dup, wg, wu, width):
    count, ff = dgate.shape
    ck = chunk_of(width, 256)
    steps = width // ck
    half = count // 2

    def kernel(_, a_ref, b_ref, g_ref, u_ref, mine_ref, near_ref):
        for lo, out in ((half, near_ref), (0, mine_ref)):
            part = dot(a_ref[lo : lo + half, :], g_ref[...], LAST)
            part += dot(b_ref[lo : lo + half, :], u_ref[...], LAST)
            out[...] = part.astype(BF16)

    out = jax.ShapeDtypeStruct((half, width), BF16)
    weights = spec((ck, ff), lambda k, s: (s[0] * steps + k, 0))
    return call(
        kernel, "inputs_back", at, steps, [dgate, dup, wg, wu],
        [fixed(dgate), fixed(dup), weights, weights],
        [out] * 2, [spec((half, ck), lambda k, s: (0, k))] * 2,
        flops=4 * count * width * ff,
    )


def weights_back(at, parts, rows, weight, hidden, dgate, dup, shapes, grads):
    arrays, tok, grd = parts
    n, width, (count, ff) = len(arrays), arrays[0].shape[1], hidden.shape
    ck = chunk_of(width, 256)
    steps = width // ck

    def kernel(_, *refs):
        xs, (w_ref, h_ref, a_ref, b_ref) = refs[:n], refs[n : n + 4]
        wg_ref, wu_ref, wd_ref = refs[-3:]
        x = stack(xs, tok, rows)
        wg_ref[...] = dot(x, a_ref[...], FIRST).astype(BF16)
        wu_ref[...] = dot(x, b_ref[...], FIRST).astype(BF16)
        g = (w_ref[...] * stack(xs, grd, rows).astype(F32)).astype(BF16)
        wd_ref[...] = dot(h_ref[...], g, FIRST).astype(BF16)

    in_specs = [spec((a.shape[0], ck), lambda k, s: (0, k)) for a in arrays]
    in_specs += [fixed(weight), fixed(hidden), fixed(dgate), fixed(dup)]
    in_specs += [pl.BlockSpec(memory_space=pl.ANY)] * len(grads)
    return call(
        kernel, "weights_back", at, steps, [*arrays, weight, hidden, dgate, dup, *grads], in_specs,
        [jax.ShapeDtypeStruct(s, BF16) for s in shapes],
        [
            spec((ck, ff), lambda k, s: (s[0] * steps + k, 0)),
            spec((ck, ff), lambda k, s: (s[0] * steps + k, 0)),
            spec((ff, ck), lambda k, s: (0, s[0] * steps + k)),
        ],
        aliases={n + 5 + i: i for i in range(len(grads))},
        flops=6 * count * width * ff,
    )


def gather_both(links, both, table, use):
    X, Y = far_masks()
    shards = lax.axis_size("tensor")
    rows = both.shape[0] // 2
    hop, xs, ys, ds, near = {0: both}, {}, {}, {}, {}
    tables, work = [table], ()
    for r in range(shards + 2):
        if r < shards - 1:
            hop[r + 1] = links.send(0, hop[r])
        if r < shards:
            xs[r] = links.send(X, hop[r])
            ys[r] = links.send(Y, hop[r])
        if r == 0:
            tables += [links.send(X, table), links.send(Y, table)]
        if r == 1:
            tables.append(links.send(Y, tables[1]))
        if r == 2:
            tables += [links.send(1, t) for t in tables]
        if 1 <= r <= shards:
            q = r - 1
            ds[q] = [links.send(Y, xs[q][:rows]), links.send(X, ys[q][rows:])]
            near[q] = [links.send(1, a) for a in (hop[q], xs[q], ys[q])]
        if 2 <= r <= shards + 1:
            q = r - 2
            near[q] += [links.send(1, a) for a in ds[q]]
            arrays = [hop[q], xs[q], ys[q]] + ds[q] + near[q]
            tok = [(0, 0), (1, 0), (2, 0), (3, 0), (5, 0), (6, 0), (7, 0), (8, 0)]
            grd = [(0, rows), (1, rows), (2, rows), (4, 0), (5, rows), (6, rows), (7, rows), (9, 0)]
            work = use(q, (arrays, tok, grd), tables)
        links.turn(*work)


def gather_plain(own, table, use):
    rows = own.shape[0] // 2
    tables = [table]
    for m in far_masks() + [1]:
        tables = tables + [swap(t, m) for t in tables]
    for j in range(lax.axis_size("tensor")):
        own = ring(own) if j else own
        pieces = [own]
        for m in far_masks() + [1]:
            pieces = pieces + [swap(p, m) for p in pieces]
        places = range(len(pieces))
        use(j, (pieces, [(i, 0) for i in places], [(i, rows) for i in places]), tables)


def plus(*terms):
    return functools.reduce(lambda a, b: a + b, [t.astype(F32) for t in terms]).astype(BF16)


def on_device(tokens, grad_out, expert_ids, gates, w_gate, w_up, w_down):
    owners, shards = lax.axis_size("expert"), lax.axis_size("tensor")
    me, z = lax.axis_index("expert"), lax.axis_index("tensor")
    rows, width = tokens.shape
    wg, wu, wd = w_gate[0], w_up[0], w_down[0]
    far = far_masks()

    chosen = expert_ids[:, :, None] == jnp.arange(owners, dtype=jnp.int32)
    table = jnp.sum(jnp.where(chosen, gates[:, :, None], 0.0), axis=1).T
    at = [lax.rem(z - j + shards, shards).reshape(1) for j in range(shards)]
    both = jnp.concatenate([tokens, grad_out])
    kept, state = [], {"sums": ()}

    def use(j, parts, tables):
        if j == 0:
            w = [lax.dynamic_index_in_dim(t, me, 0, False) for t in tables]
            state["weight"] = jnp.stack(w).reshape(-1, 1)
        kept.append(parts)
        state["sums"] = forward(
            at[j], parts, rows, state["weight"], wg, wu, wd, state["sums"], j == shards - 1
        )
        return state["sums"]

    links = Links()
    if len(far) == 2:
        gather_both(links, both, table, use)
    else:
        gather_plain(both, table, use)
    hidden, dgate, dup = state["sums"]

    order = list(range(1, shards)) + [0]
    grads = ()

    def grads_of(i, *first):
        late = [after(a, *first) for a in (hidden, dgate, dup)]
        return weights_back(
            at[i], kept[i], rows, state["weight"], *late, (wg.shape, wu.shape, wd.shape), grads
        )

    back = lambda j, *first: inputs_back(at[j], after(dgate, *first) if first else dgate, dup, wg, wu, width)
    if len(far) == 2:
        X, Y = far
        links = Links()
        n = shards
        parts, got, mine, one, two, acc, hops = {}, {}, {}, {}, {}, {}, {}
        parts[0] = back(order[0])
        done = 0
        for r in range(1, n + 4):
            if 0 <= r - 4 < n - 1:
                hops[r - 4] = links.send(0, acc[r - 4])
            if 0 <= r - 3 < n:
                q = r - 3
                m = mine[q]
                north = plus(m[2, :h], one[q][0]), m[2, h:]
                east = m[1, :h], plus(m[1, h:], one[q][1])
                two[q] = [
                    links.send(X, jnp.concatenate(east)),
                    links.send(Y, jnp.concatenate(north)),
                ]
            if 0 <= r - 2 < n:
                q = r - 2
                mine[q] = plus(parts[q][0], got[q]).reshape(-1, rows, width)
                h = rows // 2
                one[q] = [links.send(X, mine[q][3, :h]), links.send(Y, mine[q][3, h:])]
            if 0 <= r - 1 < n:
                got[r - 1] = links.send(1, parts[r - 1][1])
            last = [a for a in links.held if a.size > 1]
            if r < n:
                parts[r] = back(order[r], *last)
                links.turn(*parts[r])
            elif done < shards:
                grads = grads_of(done, *last)
                done += 1
                links.turn(*grads)
            if 0 <= r - 3 < n:
                q = r - 3
                terms = [mine[q][0], *two[q]] + ([hops[q - 1]] if q else [])
                acc[q] = plus(*terms)
        result = acc[n - 1]
        while done < shards:
            grads = grads_of(done)
            done += 1
    else:
        result = None
        for j in order:
            mine, near = back(j)
            mine = plus(mine, swap(near, 1)).reshape(-1, rows, width)
            for m in reversed(far):
                cut = mine.shape[0] // 2
                mine = plus(mine[:cut], swap(mine[cut:], m))
            terms = [mine[0]] if result is None else [mine[0], ring(result)]
            result = plus(*terms)
        for j in range(shards):
            grads = grads_of(j)
    return (result, grads[0][None], grads[1][None], grads[2][None])


def solution(mesh):
    placed = (
        P("expert", "tensor"),
        P("expert", "tensor"),
        P("expert", None),
        P("expert", None),
        P("expert", None, "tensor"),
        P("expert", None, "tensor"),
        P("expert", "tensor", None),
    )
    return jax.shard_map(
        on_device,
        mesh=mesh,
        in_specs=placed,
        out_specs=(
            P("expert", "tensor"),
            P("expert", None, "tensor"),
            P("expert", None, "tensor"),
            P("expert", "tensor", None),
        ),
        check_vma=False,
    )
```

```python
import functools
import math

import jax
import jax.numpy as jnp
from jax import lax
from jax.experimental import pallas as pl
from jax.experimental.pallas import tpu as pltpu
from jax.sharding import PartitionSpec as P

BF16 = jnp.bfloat16
F32 = jnp.float32
LAST = (((1,), (1,)), ((), ()))
FIRST = (((0,), (0,)), ((), ()))
PLAIN = (((1,), (0,)), ((), ()))
FROM = 3

dot = functools.partial(lax.dot_general, preferred_element_type=F32)


def after(a, *others):
    return lax.optimization_barrier((a,) + others)[0]


def swap(a, mask):
    n = lax.axis_size("expert")
    return lax.ppermute(a, "expert", [(i, i ^ mask) for i in range(n)])


def ring(a):
    n = lax.axis_size("tensor")
    return lax.ppermute(a, "tensor", [(i, (i + 1) % n) for i in range(n)])


class Links:
    def __init__(self):
        self.held, self.now = [], []

    def turn(self, *work):
        self.held, self.now = self.now + list(work), []

    def send(self, link, a):
        if self.held:
            a = after(a, *self.held)
        self.now.append(ring(a) if link == 0 else swap(a, link))
        return self.now[-1]


def far_masks():
    n = lax.axis_size("expert")
    return [1 << b for b in range(1, n.bit_length() - 1)]


def stack(refs, places, rows):
    return jnp.concatenate([refs[i][at : at + rows, :] for i, at in places], axis=0)


def chunk_of(width, most):
    return max(c for c in range(128, most + 1, 128) if width % c == 0)


def spec(shape, index):
    return pl.BlockSpec(shape, index)


def piece_spec(piece, ck):
    _, rows, block = piece
    return pl.BlockSpec((rows, ck), lambda k, s: (block, k))


def fixed(a):
    return pl.BlockSpec(a.shape, lambda k, s: (0,) * a.ndim)


def kept():
    return pl.BlockSpec(memory_space=pltpu.VMEM)


def call(kernel, name, at, grid, ins, in_specs, outs, out_specs, scratch=(), aliases=None, flops=0):
    moved = sum(math.prod(a.shape) * a.dtype.itemsize for a in [*ins, *outs])
    return pl.pallas_call(
        kernel,
        out_shape=outs,
        grid_spec=pltpu.PrefetchScalarGridSpec(
            num_scalar_prefetch=1,
            grid=(grid,),
            in_specs=in_specs,
            out_specs=out_specs,
            scratch_shapes=list(scratch),
        ),
        input_output_aliases=aliases or {},
        compiler_params=pltpu.CompilerParams(
            dimension_semantics=("arbitrary",), vmem_limit_bytes=48 * 2**20
        ),
        cost_estimate=pl.CostEstimate(flops=flops, bytes_accessed=moved, transcendentals=0),
        name=name,
    )(at, *ins)


def forward(at, parts, rows, weight, wg, wu, wd, sums, final):
    pieces, tok, grd = parts
    arrays = [p[0] for p in pieces]
    n, (width, ff), count = len(arrays), (arrays[0].shape[1], wg.shape[1]), len(tok) * rows
    ck = chunk_of(width, 896)
    steps = width // ck

    def kernel(_, *refs):
        xs, (w_ref, g_ref, u_ref, d_ref) = refs[:n], refs[n : n + 4]
        before, outs = refs[n + 4 : n + 4 + len(sums)], refs[n + 4 + len(sums) :]
        both, dh = outs[-2:]
        k = pl.program_id(0)

        if final or not sums:

            @pl.when(k == 0)
            def _():
                for i, acc in enumerate((both, dh)):
                    acc[...] = before[i][...] if sums else jnp.zeros_like(acc)

        x = stack(xs, tok, rows)
        both[:, :ff] += dot(x, g_ref[...], PLAIN)
        both[:, ff:] += dot(x, u_ref[...], PLAIN)
        g = (w_ref[...] * stack(xs, grd, rows).astype(F32)).astype(BF16)
        dh[...] += dot(g, d_ref[...], LAST)
        if final:

            @pl.when(k == steps - 1)
            def _():
                for i in range(count // rows):
                    here = slice(i * rows, (i + 1) * rows)
                    gate, upper, down = both[here, :ff], both[here, ff:], dh[here, :]
                    sig = jax.nn.sigmoid(gate)
                    act = gate * sig
                    outs[0][:, here] = (act * upper).T.astype(BF16)
                    slope = upper * sig * (1.0 + gate * (1.0 - sig))
                    outs[1][here, :ff] = (down * slope).astype(BF16)
                    outs[1][here, ff:] = (down * act).astype(BF16)

    accs = [(count, 2 * ff), (count, ff)]
    if final:
        outs = [pltpu.VMEM(s, BF16) for s in ((ff, count), (count, 2 * ff))]
    else:
        outs = [pltpu.VMEM(s, F32) for s in accs]
    in_specs = [piece_spec(p, ck) for p in pieces] + [
        fixed(weight),
        spec((ck, ff), lambda k, s: (s[0] * steps + k, 0)),
        spec((ck, ff), lambda k, s: (s[0] * steps + k, 0)),
        spec((ff, ck), lambda k, s: (0, s[0] * steps + k)),
    ]
    in_specs += [kept()] * len(sums)
    return call(
        kernel, "forward", at, steps, [*arrays, weight, wg, wu, wd, *sums], in_specs,
        outs, [kept() for o in outs],
        scratch=[pltpu.VMEM(s, F32) for s in accs] if final else (),
        aliases={n + 5 + i: i for i in range(len(sums))} if not final else None,
        flops=6 * count * width * ff,
    )


def inputs_back(at, grads, wg, wu, width, upper, got=None):
    count, ff = grads.shape[0], wg.shape[1]
    ck = chunk_of(width, 896)
    steps = width // ck
    half = count // 2

    def kernel(_, a_ref, g_ref, u_ref, *refs):
        part = dot(a_ref[upper * half : (upper + 1) * half, :], jnp.concatenate([g_ref[...], u_ref[...]], axis=1), LAST)
        if got is not None:
            part += refs[0][...].astype(F32)
        refs[-1][...] = part.astype(BF16)

    out = jax.ShapeDtypeStruct((half, width), BF16)
    weights = spec((ck, ff), lambda k, s: (s[0] * steps + k, 0))
    rows = spec((half, ck), lambda k, s: (0, k))
    more = [] if got is None else [got]
    return call(
        kernel, "inputs_back", at, steps, [grads, wg, wu, *more],
        [kept(), weights, weights] + [rows] * len(more),
        [out], [rows],
        flops=4 * half * width * ff,
    )[0]


def weights_back(at, parts, rows, weight, hidden, both, shapes, grads):
    pieces, tok, grd = parts
    arrays = [p[0] for p in pieces]
    n, width, (ff, count) = len(arrays), arrays[0].shape[1], hidden.shape
    ck = chunk_of(width, 896)
    steps = width // ck

    def kernel(_, *refs):
        xs, (w_ref, h_ref, b_ref) = refs[:n], refs[n : n + 3]
        wg_ref, wu_ref, wd_ref = refs[-3:]
        g = (w_ref[...] * stack(xs, grd, rows).astype(F32)).astype(BF16)
        wd_ref[...] = dot(h_ref[...], g, PLAIN).astype(BF16)
        x = stack(xs, tok, rows).T
        wg_ref[...] = dot(x, b_ref[:, :ff], PLAIN).astype(BF16)
        wu_ref[...] = dot(x, b_ref[:, ff:], PLAIN).astype(BF16)

    in_specs = [piece_spec(p, ck) for p in pieces]
    in_specs += [fixed(weight), kept(), kept()]
    in_specs += [pl.BlockSpec(memory_space=pl.ANY)] * len(grads)
    return call(
        kernel, "weights_back", at, steps, [*arrays, weight, hidden, both, *grads], in_specs,
        [jax.ShapeDtypeStruct(s, BF16) for s in shapes],
        [
            spec((ck, ff), lambda k, s: (s[0] * steps + k, 0)),
            spec((ck, ff), lambda k, s: (s[0] * steps + k, 0)),
            spec((ff, ck), lambda k, s: (0, s[0] * steps + k)),
        ],
        aliases={n + 4 + i: i for i in range(len(grads))},
        flops=6 * count * width * ff,
    )


def gather_both(links, both, table, use):
    X, Y = far_masks()
    shards = lax.axis_size("tensor")
    rows = both.shape[0] // 2
    hop, xs, ys, near = {0: both}, {}, {}, {}
    tables = [table]
    for r in range(shards + 2):
        work = ()
        if r < shards - 1:
            hop[r + 1] = links.send(0, hop[r])
        if r <= shards:
            to_x = [hop[r]] if r < shards else []
            to_y = list(to_x)
            if r:
                to_x.append(ys[r - 1][rows : 2 * rows])
                to_y.append(xs[r - 1][:rows])
            xs[r] = links.send(X, jnp.concatenate(to_x))
            ys[r] = links.send(Y, jnp.concatenate(to_y))
        if r == 0:
            tables += [links.send(X, table), links.send(Y, table)]
        if r == 1:
            tables.append(links.send(Y, tables[1]))
        if r == 2:
            tables += [links.send(1, t) for t in tables]
        if 1 <= r <= shards + 1:
            arrays = ([hop[r - 1]] if r <= shards else []) + [xs[r - 1], ys[r - 1]]
            near[r - 1] = [links.send(1, a) for a in arrays]
        if 2 <= r:
            q = r - 2
            block = 2 if q + 1 < shards else 0
            pieces = []
            for here, late in (
                ((hop[q], xs[q], ys[q]), (xs[q + 1], ys[q + 1])),
                (near[q], near[q + 1][-2:]),
            ):
                pieces += [(a, 2 * rows, 0) for a in here] + [(a, rows, block) for a in late]
            tok = [(0, 0), (1, 0), (2, 0), (4, 0), (5, 0), (6, 0), (7, 0), (9, 0)]
            grd = [(0, rows), (1, rows), (2, rows), (3, 0), (5, rows), (6, rows), (7, rows), (8, 0)]
            work = use(q, (pieces, tok, grd), tables)
        links.turn(*work)


def gather_plain(own, table, use):
    rows = own.shape[0] // 2
    tables = [table]
    for m in far_masks() + [1]:
        tables = tables + [swap(t, m) for t in tables]
    for j in range(lax.axis_size("tensor")):
        own = ring(own) if j else own
        pieces = [own]
        for m in far_masks() + [1]:
            pieces = pieces + [swap(p, m) for p in pieces]
        places = range(len(pieces))
        pieces = [(a, 2 * rows, 0) for a in pieces]
        use(j, (pieces, [(i, 0) for i in places], [(i, rows) for i in places]), tables)


def plus(*terms):
    return functools.reduce(lambda a, b: a + b, [t.astype(F32) for t in terms]).astype(BF16)


def on_device(tokens, grad_out, expert_ids, gates, w_gate, w_up, w_down):
    owners, shards = lax.axis_size("expert"), lax.axis_size("tensor")
    me, z = lax.axis_index("expert"), lax.axis_index("tensor")
    rows, width = tokens.shape
    wg, wu, wd = w_gate[0], w_up[0], w_down[0]
    far = far_masks()

    chosen = expert_ids[:, :, None] == jnp.arange(owners, dtype=jnp.int32)
    table = jnp.sum(jnp.where(chosen, gates[:, :, None], 0.0), axis=1).T
    at = [lax.rem(z - j + shards, shards).reshape(1) for j in range(shards)]
    both = jnp.concatenate([tokens, grad_out])
    kept, state = [], {"sums": ()}

    def use(j, parts, tables):
        if j == 0:
            w = [lax.dynamic_index_in_dim(t, me, 0, False) for t in tables]
            state["weight"] = jnp.stack(w).reshape(-1, 1)
        kept.append(parts)
        state["sums"] = forward(
            at[j], parts, rows, state["weight"], wg, wu, wd, state["sums"], j == shards - 1
        )
        return state["sums"]

    links = Links()
    if len(far) == 2:
        gather_both(links, both, table, use)
    else:
        gather_plain(both, table, use)
    hidden, dboth = state["sums"]

    order = list(range(1, shards)) + [0]
    grads = ()

    def grads_of(i, *first):
        late = [after(a, *first) for a in (hidden, dboth)]
        return weights_back(
            at[i], kept[i], rows, state["weight"], *late, (wg.shape, wu.shape, wd.shape), grads
        )

    def near_of(j, *first):
        late = after(dboth, *first) if first else dboth
        return inputs_back(at[j], late, wg, wu, width, 1)

    mine_of = lambda j, got: inputs_back(at[j], dboth, wg, wu, width, 0, got).reshape(-1, rows, width)
    if len(far) == 2:
        X, Y = far
        links = Links()
        n, h = shards, rows // 2
        near, got, mine, acc, hop, xs, ys = {0: near_of(order[0])}, {}, {}, {}, {}, {}, {}
        for r in range(1, n + 3):
            last = list(links.held)
            if 4 <= r:
                q = r - 4
                m = mine[q]
                from_x, from_y = xs[q + 3][:rows], ys[q + 3][:rows]
                acc[q] = plus(m[0], from_x, from_y, *([hop[q - 1]] if q else []))
                hop[q] = links.send(0, acc[q])
            to_x, to_y = [], []
            if 3 <= r:
                q = r - 3
                m, lo = mine[q], xs[r - 1].shape[0] - h
                to_x += [m[1, :h], plus(m[1, h:], ys[r - 1][lo:])]
                to_y += [plus(m[2, :h], xs[r - 1][lo:]), m[2, h:]]
            if 2 <= r <= n + 1:
                q = r - 2
                mine[q] = mine_of(order[q], got[q])
                to_x.append(mine[q][3, :h])
                to_y.append(mine[q][3, h:])
            if to_x:
                xs[r] = links.send(X, jnp.concatenate(to_x))
                ys[r] = links.send(Y, jnp.concatenate(to_y))
            if r <= n:
                got[r - 1] = links.send(1, near[r - 1])
            work = []
            if r < n:
                near[r] = near_of(order[r], *last)
                work.append(near[r])
            if r >= FROM and r - FROM < shards:
                grads = grads_of(r - FROM, *last)
                work = work + list(grads)
            links.turn(*work)
        result = plus(mine[n - 1][0], xs[n + 2][:rows], ys[n + 2][:rows], hop[n - 2])
        for i in range(max(0, n + 3 - FROM), shards):
            grads = grads_of(i)
    else:
        result = None
        for j in order:
            mine = mine_of(j, swap(near_of(j), 1))
            for m in reversed(far):
                cut = mine.shape[0] // 2
                mine = plus(mine[:cut], swap(mine[cut:], m))
            terms = [mine[0]] if result is None else [mine[0], ring(result)]
            result = plus(*terms)
        for j in range(shards):
            grads = grads_of(j)
    return (result, grads[0][None], grads[1][None], grads[2][None])


def solution(mesh):
    placed = (
        P("expert", "tensor"),
        P("expert", "tensor"),
        P("expert", None),
        P("expert", None),
        P("expert", None, "tensor"),
        P("expert", None, "tensor"),
        P("expert", "tensor", None),
    )
    return jax.shard_map(
        on_device,
        mesh=mesh,
        in_specs=placed,
        out_specs=(
            P("expert", "tensor"),
            P("expert", None, "tensor"),
            P("expert", None, "tensor"),
            P("expert", "tensor", None),
        ),
        check_vma=False,
    )
```

```python
import functools
import math

import jax
import jax.numpy as jnp
from jax import lax
from jax.experimental import pallas as pl
from jax.experimental.pallas import tpu as pltpu
from jax.sharding import PartitionSpec as P

BF16 = jnp.bfloat16
F32 = jnp.float32
LAST = (((1,), (1,)), ((), ()))
FIRST = (((0,), (0,)), ((), ()))
PLAIN = (((1,), (0,)), ((), ()))
FROM = 3
BUNDLE = 48

dot = functools.partial(lax.dot_general, preferred_element_type=F32)


def after(a, *others):
    return lax.optimization_barrier((a,) + others)[0]


def swap(a, mask):
    n = lax.axis_size("expert")
    return lax.ppermute(a, "expert", [(i, i ^ mask) for i in range(n)])


def ring(a):
    n = lax.axis_size("tensor")
    return lax.ppermute(a, "tensor", [(i, (i + 1) % n) for i in range(n)])


class Links:
    def __init__(self, loose=False):
        self.held, self.now, self.loose = [], [], loose

    def turn(self, *work):
        self.held, self.now = self.now + list(work), []

    def send(self, link, a):
        if self.held:
            a = after(a, *self.held)
        out = ring(a) if link == 0 else swap(a, link)
        if not (self.loose and link == 1):
            self.now.append(out)
        return out


def far_masks():
    n = lax.axis_size("expert")
    return [1 << b for b in range(1, n.bit_length() - 1)]


def stack(refs, places, rows):
    return jnp.concatenate([refs[i][at : at + rows, :] for i, at in places], axis=0)


def chunk_of(width, most):
    return max(c for c in range(128, most + 1, 128) if width % c == 0)


def spec(shape, index):
    return pl.BlockSpec(shape, index)


def piece_spec(piece, ck):
    _, rows, block = piece
    return pl.BlockSpec((rows, ck), lambda k, s: (block, k))


def fixed(a):
    return pl.BlockSpec(a.shape, lambda k, s: (0,) * a.ndim)


def kept():
    return pl.BlockSpec(memory_space=pltpu.VMEM)


def call(kernel, name, at, grid, ins, in_specs, outs, out_specs, scratch=(), aliases=None, flops=0):
    moved = sum(math.prod(a.shape) * a.dtype.itemsize for a in [*ins, *outs])
    return pl.pallas_call(
        kernel,
        out_shape=outs,
        grid_spec=pltpu.PrefetchScalarGridSpec(
            num_scalar_prefetch=1,
            grid=(grid,),
            in_specs=in_specs,
            out_specs=out_specs,
            scratch_shapes=list(scratch),
        ),
        input_output_aliases=aliases or {},
        compiler_params=pltpu.CompilerParams(
            dimension_semantics=("arbitrary",), vmem_limit_bytes=48 * 2**20
        ),
        cost_estimate=pl.CostEstimate(flops=flops, bytes_accessed=moved, transcendentals=0),
        name=name,
    )(at, *ins)


def forward(at, parts, rows, weight, wg, wu, wd, sums, final):
    pieces, tok, grd = parts
    arrays = [p[0] for p in pieces]
    n, (width, ff), count = len(arrays), (arrays[0].shape[1], wg.shape[1]), len(tok) * rows
    ck = chunk_of(width, 896)
    steps = width // ck

    def kernel(_, *refs):
        xs, (w_ref, g_ref, u_ref, d_ref) = refs[:n], refs[n : n + 4]
        before, outs = refs[n + 4 : n + 4 + len(sums)], refs[n + 4 + len(sums) :]
        both, dh = outs[-2:]
        k = pl.program_id(0)

        if final or not sums:

            @pl.when(k == 0)
            def _():
                for i, acc in enumerate((both, dh)):
                    acc[...] = before[i][...] if sums else jnp.zeros_like(acc)

        x = stack(xs, tok, rows)
        both[:, :ff] += dot(x, g_ref[...], PLAIN)
        both[:, ff:] += dot(x, u_ref[...], PLAIN)
        g = (w_ref[...] * stack(xs, grd, rows).astype(F32)).astype(BF16)
        dh[...] += dot(g, d_ref[...], LAST)
        if final:

            @pl.when(k == steps - 1)
            def _():
                for i in range(count // rows):
                    here = slice(i * rows, (i + 1) * rows)
                    gate, upper, down = both[here, :ff], both[here, ff:], dh[here, :]
                    sig = jax.nn.sigmoid(gate)
                    act = gate * sig
                    outs[0][:, here] = (act * upper).T.astype(BF16)
                    slope = upper * sig * (1.0 + gate * (1.0 - sig))
                    outs[1][here, :ff] = (down * slope).astype(BF16)
                    outs[1][here, ff:] = (down * act).astype(BF16)

    accs = [(count, 2 * ff), (count, ff)]
    if final:
        outs = [pltpu.VMEM(s, BF16) for s in ((ff, count), (count, 2 * ff))]
    else:
        outs = [pltpu.VMEM(s, F32) for s in accs]
    in_specs = [piece_spec(p, ck) for p in pieces] + [
        fixed(weight),
        spec((ck, ff), lambda k, s: (s[0] * steps + k, 0)),
        spec((ck, ff), lambda k, s: (s[0] * steps + k, 0)),
        spec((ff, ck), lambda k, s: (0, s[0] * steps + k)),
    ]
    in_specs += [kept()] * len(sums)
    return call(
        kernel, "forward", at, steps, [*arrays, weight, wg, wu, wd, *sums], in_specs,
        outs, [kept() for o in outs],
        scratch=[pltpu.VMEM(s, F32) for s in accs] if final else (),
        aliases={n + 5 + i: i for i in range(len(sums))} if not final else None,
        flops=6 * count * width * ff,
    )


def inputs_back(at, grads, wg, wu, width, upper, got=None):
    count, ff = grads.shape[0], wg.shape[1]
    ck = chunk_of(width, 896)
    steps = width // ck
    half = count // 2

    def kernel(_, a_ref, g_ref, u_ref, *refs):
        part = dot(a_ref[upper * half : (upper + 1) * half, :], jnp.concatenate([g_ref[...], u_ref[...]], axis=1), LAST)
        if got is not None:
            part += refs[0][...].astype(F32)
        refs[-1][...] = part.astype(BF16)

    out = jax.ShapeDtypeStruct((half, width), BF16)
    weights = spec((ck, ff), lambda k, s: (s[0] * steps + k, 0))
    rows = spec((half, ck), lambda k, s: (0, k))
    more = [] if got is None else [got]
    return call(
        kernel, "inputs_back", at, steps, [grads, wg, wu, *more],
        [kept(), weights, weights] + [rows] * len(more),
        [out], [rows],
        flops=4 * half * width * ff,
    )[0]


def weights_back(at, parts, rows, weight, hidden, both, shapes, grads):
    pieces, tok, grd = parts
    arrays = [p[0] for p in pieces]
    n, width, (ff, count) = len(arrays), arrays[0].shape[1], hidden.shape
    ck = chunk_of(width, 896)
    steps = width // ck

    def kernel(_, *refs):
        xs, (w_ref, h_ref, b_ref) = refs[:n], refs[n : n + 3]
        wg_ref, wu_ref, wd_ref = refs[-3:]
        g = (w_ref[...] * stack(xs, grd, rows).astype(F32)).astype(BF16)
        wd_ref[...] = dot(h_ref[...], g, PLAIN).astype(BF16)
        x = stack(xs, tok, rows).T
        wg_ref[...] = dot(x, b_ref[:, :ff], PLAIN).astype(BF16)
        wu_ref[...] = dot(x, b_ref[:, ff:], PLAIN).astype(BF16)

    in_specs = [piece_spec(p, ck) for p in pieces]
    in_specs += [fixed(weight), kept(), kept()]
    in_specs += [pl.BlockSpec(memory_space=pl.ANY)] * len(grads)
    return call(
        kernel, "weights_back", at, steps, [*arrays, weight, hidden, both, *grads], in_specs,
        [jax.ShapeDtypeStruct(s, BF16) for s in shapes],
        [
            spec((ck, ff), lambda k, s: (s[0] * steps + k, 0)),
            spec((ck, ff), lambda k, s: (s[0] * steps + k, 0)),
            spec((ff, ck), lambda k, s: (0, s[0] * steps + k)),
        ],
        aliases={n + 4 + i: i for i in range(len(grads))},
        flops=6 * count * width * ff,
    )


def bundle(own, x, y, rows):
    n, width = own.shape
    ck = chunk_of(width, 896)

    def kernel(own_ref, x_ref, y_ref, to_x_ref, to_y_ref):
        for out, more in ((to_x_ref, y_ref), (to_y_ref, x_ref)):
            out[:n, :] = own_ref[...]
            out[n:, :] = more[...]

    out = jax.ShapeDtypeStruct((n + rows, width), own.dtype)
    whole = spec((n + rows, ck), lambda k: (0, k))
    return pl.pallas_call(
        kernel,
        out_shape=[out, out],
        grid=(width // ck,),
        in_specs=[
            spec((n, ck), lambda k: (0, k)),
            spec((rows, ck), lambda k: (0, k)),
            spec((rows, ck), lambda k: (1, k)),
        ],
        out_specs=[whole, whole],
        compiler_params=pltpu.CompilerParams(vmem_limit_bytes=BUNDLE * 2**20),
        cost_estimate=pl.CostEstimate(flops=0, bytes_accessed=4 * out.size * 2, transcendentals=0),
        name="bundle",
    )(own, x, y)


def gather_both(links, both, table, use):
    X, Y = far_masks()
    shards = lax.axis_size("tensor")
    rows = both.shape[0] // 2
    hop, xs, ys, near = {0: both}, {}, {}, {}
    tables = [table]
    for r in range(shards + 2):
        work = ()
        if r < shards - 1:
            hop[r + 1] = links.send(0, hop[r])
        if r <= shards:
            if r == 0:
                to_x = to_y = both
            elif r < shards:
                to_x, to_y = bundle(hop[r], xs[r - 1], ys[r - 1], rows)
            else:
                to_x, to_y = ys[r - 1][rows : 2 * rows], xs[r - 1][:rows]
            xs[r] = links.send(X, to_x)
            ys[r] = links.send(Y, to_y)
        if r == 0:
            tables += [links.send(X, table), links.send(Y, table)]
        if r == 1:
            tables.append(links.send(Y, tables[1]))
        if r == 2:
            tables += list(links.send(1, jnp.stack(tables)))
        if 1 <= r <= shards + 1:
            arrays = ([hop[r - 1]] if r <= shards else []) + [xs[r - 1], ys[r - 1]]
            near[r - 1] = [links.send(1, a) for a in arrays]
        if 2 <= r:
            q = r - 2
            block = 2 if q + 1 < shards else 0
            pieces = []
            for here, late in (
                ((hop[q], xs[q], ys[q]), (xs[q + 1], ys[q + 1])),
                (near[q], near[q + 1][-2:]),
            ):
                pieces += [(a, 2 * rows, 0) for a in here] + [(a, rows, block) for a in late]
            tok = [(0, 0), (1, 0), (2, 0), (4, 0), (5, 0), (6, 0), (7, 0), (9, 0)]
            grd = [(0, rows), (1, rows), (2, rows), (3, 0), (5, rows), (6, rows), (7, rows), (8, 0)]
            work = use(q, (pieces, tok, grd), tables)
        links.turn(*work)


def gather_plain(own, table, use):
    rows = own.shape[0] // 2
    tables = [table]
    for m in far_masks() + [1]:
        tables = tables + [swap(t, m) for t in tables]
    for j in range(lax.axis_size("tensor")):
        own = ring(own) if j else own
        pieces = [own]
        for m in far_masks() + [1]:
            pieces = pieces + [swap(p, m) for p in pieces]
        places = range(len(pieces))
        pieces = [(a, 2 * rows, 0) for a in pieces]
        use(j, (pieces, [(i, 0) for i in places], [(i, rows) for i in places]), tables)


def plus(*terms):
    return functools.reduce(lambda a, b: a + b, [t.astype(F32) for t in terms]).astype(BF16)


def on_device(tokens, grad_out, expert_ids, gates, w_gate, w_up, w_down):
    owners, shards = lax.axis_size("expert"), lax.axis_size("tensor")
    me, z = lax.axis_index("expert"), lax.axis_index("tensor")
    rows, width = tokens.shape
    wg, wu, wd = w_gate[0], w_up[0], w_down[0]
    far = far_masks()

    chosen = expert_ids[:, :, None] == jnp.arange(owners, dtype=jnp.int32)
    table = jnp.sum(jnp.where(chosen, gates[:, :, None], 0.0), axis=1).T
    at = [lax.rem(z - j + shards, shards).reshape(1) for j in range(shards)]
    both = jnp.concatenate([tokens, grad_out])
    kept, state = [], {"sums": ()}

    def use(j, parts, tables):
        if j == 0:
            w = [lax.dynamic_index_in_dim(t, me, 0, False) for t in tables]
            state["weight"] = jnp.stack(w).reshape(-1, 1)
        kept.append(parts)
        state["sums"] = forward(
            at[j], parts, rows, state["weight"], wg, wu, wd, state["sums"], j == shards - 1
        )
        return state["sums"]

    links = Links(True)
    if len(far) == 2:
        gather_both(links, both, table, use)
    else:
        gather_plain(both, table, use)
    hidden, dboth = state["sums"]

    order = list(range(1, shards)) + [0]
    grads = ()

    def grads_of(i, *first):
        late = [after(a, *first) for a in (hidden, dboth)]
        return weights_back(
            at[i], kept[i], rows, state["weight"], *late, (wg.shape, wu.shape, wd.shape), grads
        )

    def near_of(j, *first):
        late = after(dboth, *first) if first else dboth
        return inputs_back(at[j], late, wg, wu, width, 1)

    mine_of = lambda j, got: inputs_back(at[j], dboth, wg, wu, width, 0, got).reshape(-1, rows, width)
    if len(far) == 2:
        X, Y = far
        links = Links()
        n, h = shards, rows // 2
        near, got, mine, acc, hop, xs, ys = {0: near_of(order[0])}, {}, {}, {}, {}, {}, {}
        for r in range(1, n + 3):
            last = list(links.held)
            if 4 <= r:
                q = r - 4
                m = mine[q]
                from_x, from_y = xs[q + 3][:rows], ys[q + 3][:rows]
                acc[q] = plus(m[0], from_x, from_y, *([hop[q - 1]] if q else []))
                hop[q] = links.send(0, acc[q])
            to_x, to_y = [], []
            if 3 <= r:
                q = r - 3
                m, lo = mine[q], xs[r - 1].shape[0] - h
                to_x += [m[1, :h], plus(m[1, h:], ys[r - 1][lo:])]
                to_y += [plus(m[2, :h], xs[r - 1][lo:]), m[2, h:]]
            if 2 <= r <= n + 1:
                q = r - 2
                mine[q] = mine_of(order[q], got[q])
                to_x.append(mine[q][3, :h])
                to_y.append(mine[q][3, h:])
            if to_x:
                xs[r] = links.send(X, jnp.concatenate(to_x))
                ys[r] = links.send(Y, jnp.concatenate(to_y))
            if r <= n:
                got[r - 1] = links.send(1, near[r - 1])
            work = []
            if r < n:
                near[r] = near_of(order[r], *last)
                work.append(near[r])
            if r >= FROM and r - FROM < shards:
                grads = grads_of(r - FROM, *last)
                work = work + list(grads)
            links.turn(*work)
        result = plus(mine[n - 1][0], xs[n + 2][:rows], ys[n + 2][:rows], hop[n - 2])
        for i in range(max(0, n + 3 - FROM), shards):
            grads = grads_of(i)
    else:
        result = None
        for j in order:
            mine = mine_of(j, swap(near_of(j), 1))
            for m in reversed(far):
                cut = mine.shape[0] // 2
                mine = plus(mine[:cut], swap(mine[cut:], m))
            terms = [mine[0]] if result is None else [mine[0], ring(result)]
            result = plus(*terms)
        for j in range(shards):
            grads = grads_of(j)
    return (result, grads[0][None], grads[1][None], grads[2][None])


def solution(mesh):
    placed = (
        P("expert", "tensor"),
        P("expert", "tensor"),
        P("expert", None),
        P("expert", None),
        P("expert", None, "tensor"),
        P("expert", None, "tensor"),
        P("expert", "tensor", None),
    )
    return jax.shard_map(
        on_device,
        mesh=mesh,
        in_specs=placed,
        out_specs=(
            P("expert", "tensor"),
            P("expert", None, "tensor"),
            P("expert", None, "tensor"),
            P("expert", "tensor", None),
        ),
        check_vma=False,
    )
```

```python
import functools
import math

import jax
import jax.numpy as jnp
from jax import lax
from jax.experimental import pallas as pl
from jax.experimental.pallas import tpu as pltpu
from jax.sharding import PartitionSpec as P

BF16 = jnp.bfloat16
F32 = jnp.float32
LAST = (((1,), (1,)), ((), ()))
FIRST = (((0,), (0,)), ((), ()))
PLAIN = (((1,), (0,)), ((), ()))
FROM = 3
BUNDLE = 48

dot = functools.partial(lax.dot_general, preferred_element_type=F32)


def after(a, *others):
    return lax.optimization_barrier((a,) + others)[0]


def swap(a, mask):
    n = lax.axis_size("expert")
    return lax.ppermute(a, "expert", [(i, i ^ mask) for i in range(n)])


def ring(a):
    n = lax.axis_size("tensor")
    return lax.ppermute(a, "tensor", [(i, (i + 1) % n) for i in range(n)])


class Links:
    def __init__(self, loose=False):
        self.held, self.now, self.loose = [], [], loose

    def turn(self, *work):
        self.held, self.now = self.now + list(work), []

    def send(self, link, a):
        if self.held:
            a = after(a, *self.held)
        out = ring(a) if link == 0 else swap(a, link)
        if not (self.loose and link == 1):
            self.now.append(out)
        return out


def far_masks():
    n = lax.axis_size("expert")
    return [1 << b for b in range(1, n.bit_length() - 1)]


def stack(refs, places, rows):
    return jnp.concatenate([refs[i][at : at + rows, :] for i, at in places], axis=0)


def chunk_of(width, most):
    return max(c for c in range(128, most + 1, 128) if width % c == 0)


def spec(shape, index):
    return pl.BlockSpec(shape, index)


def piece_spec(piece, ck):
    _, rows, block = piece
    return pl.BlockSpec((rows, ck), lambda k, s: (block, k))


def fixed(a):
    return pl.BlockSpec(a.shape, lambda k, s: (0,) * a.ndim)


def kept():
    return pl.BlockSpec(memory_space=pltpu.VMEM)


def call(kernel, name, at, grid, ins, in_specs, outs, out_specs, scratch=(), aliases=None, flops=0):
    moved = sum(math.prod(a.shape) * a.dtype.itemsize for a in [*ins, *outs])
    return pl.pallas_call(
        kernel,
        out_shape=outs,
        grid_spec=pltpu.PrefetchScalarGridSpec(
            num_scalar_prefetch=1,
            grid=(grid,),
            in_specs=in_specs,
            out_specs=out_specs,
            scratch_shapes=list(scratch),
        ),
        input_output_aliases=aliases or {},
        compiler_params=pltpu.CompilerParams(
            dimension_semantics=("arbitrary",), vmem_limit_bytes=48 * 2**20
        ),
        cost_estimate=pl.CostEstimate(flops=flops, bytes_accessed=moved, transcendentals=0),
        name=name,
    )(at, *ins)


def forward(at, parts, rows, weight, wg, wu, wd, sums, final):
    pieces, tok, grd = parts
    arrays = [p[0] for p in pieces]
    n, (width, ff), count = len(arrays), (arrays[0].shape[1], wg.shape[1]), len(tok) * rows
    ck = chunk_of(width, 1792)
    steps = width // ck

    def kernel(_, *refs):
        xs, (w_ref, g_ref, u_ref, d_ref) = refs[:n], refs[n : n + 4]
        before, outs = refs[n + 4 : n + 4 + len(sums)], refs[n + 4 + len(sums) :]
        both, dh = outs[-2:]
        k = pl.program_id(0)

        if final or not sums:

            @pl.when(k == 0)
            def _():
                for i, acc in enumerate((both, dh)):
                    acc[...] = before[i][...] if sums else jnp.zeros_like(acc)

        x = stack(xs, tok, rows)
        both[:, :ff] += dot(x, g_ref[...], PLAIN)
        both[:, ff:] += dot(x, u_ref[...], PLAIN)
        g = (w_ref[...] * stack(xs, grd, rows).astype(F32)).astype(BF16)
        dh[...] += dot(g, d_ref[...], LAST)
        if final:

            @pl.when(k == steps - 1)
            def _():
                for i in range(count // rows):
                    here = slice(i * rows, (i + 1) * rows)
                    gate, upper, down = both[here, :ff], both[here, ff:], dh[here, :]
                    sig = jax.nn.sigmoid(gate)
                    act = gate * sig
                    outs[0][:, here] = (act * upper).T.astype(BF16)
                    slope = upper * sig * (1.0 + gate * (1.0 - sig))
                    outs[1][here, :ff] = (down * slope).astype(BF16)
                    outs[1][here, ff:] = (down * act).astype(BF16)

    accs = [(count, 2 * ff), (count, ff)]
    if final:
        outs = [pltpu.VMEM(s, BF16) for s in ((ff, count), (count, 2 * ff))]
    else:
        outs = [pltpu.VMEM(s, F32) for s in accs]
    in_specs = [piece_spec(p, ck) for p in pieces] + [
        fixed(weight),
        spec((ck, ff), lambda k, s: (s[0] * steps + k, 0)),
        spec((ck, ff), lambda k, s: (s[0] * steps + k, 0)),
        spec((ff, ck), lambda k, s: (0, s[0] * steps + k)),
    ]
    in_specs += [kept()] * len(sums)
    return call(
        kernel, "forward", at, steps, [*arrays, weight, wg, wu, wd, *sums], in_specs,
        outs, [kept() for o in outs],
        scratch=[pltpu.VMEM(s, F32) for s in accs] if final else (),
        aliases={n + 5 + i: i for i in range(len(sums))} if not final else None,
        flops=6 * count * width * ff,
    )


def inputs_back(at, grads, wg, wu, width, upper, got=None):
    count, ff = grads.shape[0], wg.shape[1]
    ck = chunk_of(width, 896)
    steps = width // ck
    half = count // 2

    def kernel(_, a_ref, g_ref, u_ref, *refs):
        part = dot(a_ref[upper * half : (upper + 1) * half, :], jnp.concatenate([g_ref[...], u_ref[...]], axis=1), LAST)
        if got is not None:
            part += refs[0][...].astype(F32)
        refs[-1][...] = part.astype(BF16)

    out = jax.ShapeDtypeStruct((half, width), BF16)
    weights = spec((ck, ff), lambda k, s: (s[0] * steps + k, 0))
    rows = spec((half, ck), lambda k, s: (0, k))
    more = [] if got is None else [got]
    return call(
        kernel, "inputs_back", at, steps, [grads, wg, wu, *more],
        [kept(), weights, weights] + [rows] * len(more),
        [out], [rows],
        flops=4 * half * width * ff,
    )[0]


def weights_back(at, parts, rows, weight, hidden, both, shapes, grads):
    pieces, tok, grd = parts
    arrays = [p[0] for p in pieces]
    n, width, (ff, count) = len(arrays), arrays[0].shape[1], hidden.shape
    ck = chunk_of(width, 896)
    steps = width // ck

    def kernel(_, *refs):
        xs, (w_ref, h_ref, b_ref) = refs[:n], refs[n : n + 3]
        wg_ref, wu_ref, wd_ref = refs[-3:]
        g = (w_ref[...] * stack(xs, grd, rows).astype(F32)).astype(BF16)
        wd_ref[...] = dot(h_ref[...], g, PLAIN).astype(BF16)
        x = stack(xs, tok, rows).T
        wg_ref[...] = dot(x, b_ref[:, :ff], PLAIN).astype(BF16)
        wu_ref[...] = dot(x, b_ref[:, ff:], PLAIN).astype(BF16)

    in_specs = [piece_spec(p, ck) for p in pieces]
    in_specs += [fixed(weight), kept(), kept()]
    in_specs += [pl.BlockSpec(memory_space=pl.ANY)] * len(grads)
    return call(
        kernel, "weights_back", at, steps, [*arrays, weight, hidden, both, *grads], in_specs,
        [jax.ShapeDtypeStruct(s, BF16) for s in shapes],
        [
            spec((ck, ff), lambda k, s: (s[0] * steps + k, 0)),
            spec((ck, ff), lambda k, s: (s[0] * steps + k, 0)),
            spec((ff, ck), lambda k, s: (0, s[0] * steps + k)),
        ],
        aliases={n + 4 + i: i for i in range(len(grads))},
        flops=6 * count * width * ff,
    )


def bundle(own, x, y, rows):
    n, width = own.shape
    ck = chunk_of(width, 896)

    def kernel(own_ref, x_ref, y_ref, to_x_ref, to_y_ref):
        for out, more in ((to_x_ref, y_ref), (to_y_ref, x_ref)):
            out[:n, :] = own_ref[...]
            out[n:, :] = more[...]

    out = jax.ShapeDtypeStruct((n + rows, width), own.dtype)
    whole = spec((n + rows, ck), lambda k: (0, k))
    return pl.pallas_call(
        kernel,
        out_shape=[out, out],
        grid=(width // ck,),
        in_specs=[
            spec((n, ck), lambda k: (0, k)),
            spec((rows, ck), lambda k: (0, k)),
            spec((rows, ck), lambda k: (1, k)),
        ],
        out_specs=[whole, whole],
        compiler_params=pltpu.CompilerParams(vmem_limit_bytes=BUNDLE * 2**20),
        cost_estimate=pl.CostEstimate(flops=0, bytes_accessed=4 * out.size * 2, transcendentals=0),
        name="bundle",
    )(own, x, y)


def onward(mine, xs, ys, later):
    _, rows, width = mine.shape
    h, ck = rows // 2, chunk_of(width, 896)

    def kernel(e_ref, n_ref, x_ref, y_ref, *refs):
        to_x_ref, to_y_ref = refs[-2:]
        to_x_ref[:h, :] = e_ref[0, :h, :]
        to_x_ref[h:rows, :] = (e_ref[0, h:, :].astype(F32) + y_ref[...].astype(F32)).astype(BF16)
        to_y_ref[:h, :] = (n_ref[0, :h, :].astype(F32) + x_ref[...].astype(F32)).astype(BF16)
        to_y_ref[h:rows, :] = n_ref[0, h:, :]
        if later is not None:
            to_x_ref[rows:, :] = refs[0][0, :h, :]
            to_y_ref[rows:, :] = refs[0][0, h:, :]

    more = [] if later is None else [later]
    end = xs.shape[0] // h - 1
    out = jax.ShapeDtypeStruct((rows + h * len(more), width), BF16)
    block = lambda i: spec((1, rows, ck), lambda k: (i, 0, k))
    half = spec((h, ck), lambda k: (end, k))
    whole = spec((out.shape[0], ck), lambda k: (0, k))
    return pl.pallas_call(
        kernel,
        out_shape=[out, out],
        grid=(width // ck,),
        in_specs=[block(1), block(2), half, half] + [block(3)] * len(more),
        out_specs=[whole, whole],
        compiler_params=pltpu.CompilerParams(vmem_limit_bytes=BUNDLE * 2**20),
        cost_estimate=pl.CostEstimate(flops=0, bytes_accessed=8 * out.size, transcendentals=0),
        name="onward",
    )(mine, mine, xs, ys, *more)


def gather_both(links, both, table, use):
    X, Y = far_masks()
    shards = lax.axis_size("tensor")
    rows = both.shape[0] // 2
    hop, xs, ys, near = {0: both}, {}, {}, {}
    tables = [table]
    for r in range(shards + 2):
        work = ()
        if r < shards - 1:
            hop[r + 1] = links.send(0, hop[r])
        if r <= shards:
            if r == 0:
                to_x = to_y = both
            elif r < shards:
                to_x, to_y = bundle(hop[r], xs[r - 1], ys[r - 1], rows)
            else:
                to_x, to_y = ys[r - 1][rows : 2 * rows], xs[r - 1][:rows]
            xs[r] = links.send(X, to_x)
            ys[r] = links.send(Y, to_y)
        if r == 0:
            tables += [links.send(X, table), links.send(Y, table)]
        if r == 1:
            tables.append(links.send(Y, tables[1]))
        if r == 2:
            tables += list(links.send(1, jnp.stack(tables)))
        if 1 <= r <= shards + 1:
            arrays = ([hop[r - 1]] if r <= shards else []) + [xs[r - 1], ys[r - 1]]
            near[r - 1] = [links.send(1, a) for a in arrays]
        if 2 <= r:
            q = r - 2
            block = 2 if q + 1 < shards else 0
            pieces = []
            for here, late in (
                ((hop[q], xs[q], ys[q]), (xs[q + 1], ys[q + 1])),
                (near[q], near[q + 1][-2:]),
            ):
                pieces += [(a, 2 * rows, 0) for a in here] + [(a, rows, block) for a in late]
            tok = [(0, 0), (1, 0), (2, 0), (4, 0), (5, 0), (6, 0), (7, 0), (9, 0)]
            grd = [(0, rows), (1, rows), (2, rows), (3, 0), (5, rows), (6, rows), (7, rows), (8, 0)]
            work = use(q, (pieces, tok, grd), tables)
        links.turn(*work)


def gather_plain(own, table, use):
    rows = own.shape[0] // 2
    tables = [table]
    for m in far_masks() + [1]:
        tables = tables + [swap(t, m) for t in tables]
    for j in range(lax.axis_size("tensor")):
        own = ring(own) if j else own
        pieces = [own]
        for m in far_masks() + [1]:
            pieces = pieces + [swap(p, m) for p in pieces]
        places = range(len(pieces))
        pieces = [(a, 2 * rows, 0) for a in pieces]
        use(j, (pieces, [(i, 0) for i in places], [(i, rows) for i in places]), tables)


def plus(*terms):
    return functools.reduce(lambda a, b: a + b, [t.astype(F32) for t in terms]).astype(BF16)


def on_device(tokens, grad_out, expert_ids, gates, w_gate, w_up, w_down):
    owners, shards = lax.axis_size("expert"), lax.axis_size("tensor")
    me, z = lax.axis_index("expert"), lax.axis_index("tensor")
    rows, width = tokens.shape
    wg, wu, wd = w_gate[0], w_up[0], w_down[0]
    far = far_masks()

    chosen = expert_ids[:, :, None] == jnp.arange(owners, dtype=jnp.int32)
    table = jnp.sum(jnp.where(chosen, gates[:, :, None], 0.0), axis=1).T
    at = [lax.rem(z - j + shards, shards).reshape(1) for j in range(shards)]
    both = jnp.concatenate([tokens, grad_out])
    kept, state = [], {"sums": ()}

    def use(j, parts, tables):
        if j == 0:
            w = [lax.dynamic_index_in_dim(t, me, 0, False) for t in tables]
            state["weight"] = jnp.stack(w).reshape(-1, 1)
        kept.append(parts)
        state["sums"] = forward(
            at[j], parts, rows, state["weight"], wg, wu, wd, state["sums"], j == shards - 1
        )
        return state["sums"]

    links = Links(True)
    if len(far) == 2:
        gather_both(links, both, table, use)
    else:
        gather_plain(both, table, use)
    hidden, dboth = state["sums"]

    order = list(range(1, shards)) + [0]
    grads = ()

    def grads_of(i, *first):
        late = [after(a, *first) for a in (hidden, dboth)]
        return weights_back(
            at[i], kept[i], rows, state["weight"], *late, (wg.shape, wu.shape, wd.shape), grads
        )

    def near_of(j, *first):
        late = after(dboth, *first) if first else dboth
        return inputs_back(at[j], late, wg, wu, width, 1)

    mine_of = lambda j, got: inputs_back(at[j], dboth, wg, wu, width, 0, got).reshape(-1, rows, width)
    if len(far) == 2:
        X, Y = far
        links = Links()
        n, h = shards, rows // 2
        near, got, mine, acc, hop, xs, ys = {0: near_of(order[0])}, {}, {}, {}, {}, {}, {}
        for r in range(1, n + 3):
            last = list(links.held)
            if 4 <= r:
                q = r - 4
                m = mine[q]
                from_x, from_y = xs[q + 3][:rows], ys[q + 3][:rows]
                acc[q] = plus(m[0], from_x, from_y, *([hop[q - 1]] if q else []))
                hop[q] = links.send(0, acc[q])
            if 2 <= r <= n + 1:
                mine[r - 2] = mine_of(order[r - 2], got[r - 2])
            if 3 <= r:
                to_x, to_y = onward(mine[r - 3], xs[r - 1], ys[r - 1], mine.get(r - 2))
            elif r == 2:
                to_x, to_y = mine[0][3, :h], mine[0][3, h:]
            if 2 <= r:
                xs[r] = links.send(X, to_x)
                ys[r] = links.send(Y, to_y)
            if r <= n:
                got[r - 1] = links.send(1, near[r - 1])
            work = []
            if r < n:
                near[r] = near_of(order[r], *last)
                work.append(near[r])
            if r >= FROM and r - FROM < shards:
                grads = grads_of(r - FROM, *last)
                work = work + list(grads)
            links.turn(*work)
        result = plus(mine[n - 1][0], xs[n + 2][:rows], ys[n + 2][:rows], hop[n - 2])
        for i in range(max(0, n + 3 - FROM), shards):
            grads = grads_of(i)
    else:
        result = None
        for j in order:
            mine = mine_of(j, swap(near_of(j), 1))
            for m in reversed(far):
                cut = mine.shape[0] // 2
                mine = plus(mine[:cut], swap(mine[cut:], m))
            terms = [mine[0]] if result is None else [mine[0], ring(result)]
            result = plus(*terms)
        for j in range(shards):
            grads = grads_of(j)
    return (result, grads[0][None], grads[1][None], grads[2][None])


def solution(mesh):
    placed = (
        P("expert", "tensor"),
        P("expert", "tensor"),
        P("expert", None),
        P("expert", None),
        P("expert", None, "tensor"),
        P("expert", None, "tensor"),
        P("expert", "tensor", None),
    )
    return jax.shard_map(
        on_device,
        mesh=mesh,
        in_specs=placed,
        out_specs=(
            P("expert", "tensor"),
            P("expert", None, "tensor"),
            P("expert", None, "tensor"),
            P("expert", "tensor", None),
        ),
        check_vma=False,
    )
```

```python
import functools
import math

import jax
import jax.numpy as jnp
from jax import lax
from jax.experimental import pallas as pl
from jax.experimental.pallas import tpu as pltpu
from jax.sharding import PartitionSpec as P

BF16 = jnp.bfloat16
F32 = jnp.float32
LAST = (((1,), (1,)), ((), ()))
FIRST = (((0,), (0,)), ((), ()))
PLAIN = (((1,), (0,)), ((), ()))
FROM = 3
BUNDLE = 48

dot = functools.partial(lax.dot_general, preferred_element_type=F32)


def after(a, *others):
    return lax.optimization_barrier((a,) + others)[0]


def swap(a, mask):
    n = lax.axis_size("expert")
    return lax.ppermute(a, "expert", [(i, i ^ mask) for i in range(n)])


def ring(a):
    n = lax.axis_size("tensor")
    return lax.ppermute(a, "tensor", [(i, (i + 1) % n) for i in range(n)])


class Links:
    def __init__(self, loose=False):
        self.held, self.now, self.loose = [], [], loose

    def turn(self, *work):
        self.held, self.now = self.now + list(work), []

    def send(self, link, a):
        if self.held:
            a = after(a, *self.held)
        out = ring(a) if link == 0 else swap(a, link)
        if not (self.loose and link == 1):
            self.now.append(out)
        return out


def far_masks():
    n = lax.axis_size("expert")
    return [1 << b for b in range(1, n.bit_length() - 1)]


def stack(refs, places, rows):
    return jnp.concatenate([refs[i][at : at + rows, :] for i, at in places], axis=0)


def chunk_of(width, most):
    return max(c for c in range(128, most + 1, 128) if width % c == 0)


def spec(shape, index):
    return pl.BlockSpec(shape, index)


def piece_spec(piece, ck):
    _, rows, block = piece
    return pl.BlockSpec((rows, ck), lambda k, s: (block, k))


def fixed(a):
    return pl.BlockSpec(a.shape, lambda k, s: (0,) * a.ndim)


def kept():
    return pl.BlockSpec(memory_space=pltpu.VMEM)


def call(kernel, name, at, grid, ins, in_specs, outs, out_specs, scratch=(), aliases=None, flops=0):
    moved = sum(math.prod(a.shape) * a.dtype.itemsize for a in [*ins, *outs])
    return pl.pallas_call(
        kernel,
        out_shape=outs,
        grid_spec=pltpu.PrefetchScalarGridSpec(
            num_scalar_prefetch=1,
            grid=(grid,),
            in_specs=in_specs,
            out_specs=out_specs,
            scratch_shapes=list(scratch),
        ),
        input_output_aliases=aliases or {},
        compiler_params=pltpu.CompilerParams(
            dimension_semantics=("arbitrary",), vmem_limit_bytes=48 * 2**20
        ),
        cost_estimate=pl.CostEstimate(flops=flops, bytes_accessed=moved, transcendentals=0),
        name=name,
    )(at, *ins)


def forward(at, parts, rows, weight, wg, wu, wd, sums, final):
    pieces, tok, grd = parts
    arrays = [p[0] for p in pieces]
    n, (width, ff), count = len(arrays), (arrays[0].shape[1], wg.shape[1]), len(tok) * rows
    ck = chunk_of(width, 1792)
    steps = width // ck

    def kernel(_, *refs):
        xs, (w_ref, g_ref, u_ref, d_ref) = refs[:n], refs[n : n + 4]
        before, outs = refs[n + 4 : n + 4 + len(sums)], refs[n + 4 + len(sums) :]
        both, dh = outs[-2:]
        k = pl.program_id(0)

        if final or not sums:

            @pl.when(k == 0)
            def _():
                for i, acc in enumerate((both, dh)):
                    acc[...] = before[i][...] if sums else jnp.zeros_like(acc)

        x = stack(xs, tok, rows)
        both[:, :ff] += dot(x, g_ref[...], PLAIN)
        both[:, ff:] += dot(x, u_ref[...], PLAIN)
        g = (w_ref[...] * stack(xs, grd, rows).astype(F32)).astype(BF16)
        dh[...] += dot(g, d_ref[...], LAST)
        if final:

            @pl.when(k == steps - 1)
            def _():
                for i in range(count // rows):
                    here = slice(i * rows, (i + 1) * rows)
                    gate, upper, down = both[here, :ff], both[here, ff:], dh[here, :]
                    sig = jax.nn.sigmoid(gate)
                    act = gate * sig
                    outs[0][:, here] = (act * upper).T.astype(BF16)
                    slope = upper * sig * (1.0 + gate * (1.0 - sig))
                    outs[1][here, :ff] = (down * slope).astype(BF16)
                    outs[1][here, ff:] = (down * act).astype(BF16)

    accs = [(count, 2 * ff), (count, ff)]
    if final:
        outs = [pltpu.VMEM(s, BF16) for s in ((ff, count), (count, 2 * ff))]
    else:
        outs = [pltpu.VMEM(s, F32) for s in accs]
    in_specs = [piece_spec(p, ck) for p in pieces] + [
        fixed(weight),
        spec((ck, ff), lambda k, s: (s[0] * steps + k, 0)),
        spec((ck, ff), lambda k, s: (s[0] * steps + k, 0)),
        spec((ff, ck), lambda k, s: (0, s[0] * steps + k)),
    ]
    in_specs += [kept()] * len(sums)
    return call(
        kernel, "forward", at, steps, [*arrays, weight, wg, wu, wd, *sums], in_specs,
        outs, [kept() for o in outs],
        scratch=[pltpu.VMEM(s, F32) for s in accs] if final else (),
        aliases={n + 5 + i: i for i in range(len(sums))} if not final else None,
        flops=6 * count * width * ff,
    )


def inputs_back(at, grads, wg, wu, width, upper, got=None):
    count, ff = grads.shape[0], wg.shape[1]
    ck = chunk_of(width, 896)
    steps = width // ck
    half = count // 2

    def kernel(_, a_ref, g_ref, u_ref, *refs):
        part = dot(a_ref[upper * half : (upper + 1) * half, :], jnp.concatenate([g_ref[...], u_ref[...]], axis=1), LAST)
        if got is not None:
            part += refs[0][...].astype(F32)
        refs[-1][...] = part.astype(BF16)

    out = jax.ShapeDtypeStruct((half, width), BF16)
    weights = spec((ck, ff), lambda k, s: (s[0] * steps + k, 0))
    rows = spec((half, ck), lambda k, s: (0, k))
    more = [] if got is None else [got]
    return call(
        kernel, "inputs_back", at, steps, [grads, wg, wu, *more],
        [kept(), weights, weights] + [rows] * len(more),
        [out], [rows],
        flops=4 * half * width * ff,
    )[0]


def weights_back(at, parts, rows, weight, hidden, both, shapes, grads):
    pieces, tok, grd = parts
    arrays = [p[0] for p in pieces]
    n, width, (ff, count) = len(arrays), arrays[0].shape[1], hidden.shape
    ck = chunk_of(width, 896)
    steps = width // ck

    def kernel(_, *refs):
        xs, (w_ref, h_ref, b_ref) = refs[:n], refs[n : n + 3]
        wg_ref, wu_ref, wd_ref = refs[-3:]
        g = (w_ref[...] * stack(xs, grd, rows).astype(F32)).astype(BF16)
        wd_ref[...] = dot(h_ref[...], g, PLAIN).astype(BF16)
        x = stack(xs, tok, rows).T
        wg_ref[...] = dot(x, b_ref[:, :ff], PLAIN).astype(BF16)
        wu_ref[...] = dot(x, b_ref[:, ff:], PLAIN).astype(BF16)

    in_specs = [piece_spec(p, ck) for p in pieces]
    in_specs += [fixed(weight), kept(), kept()]
    in_specs += [pl.BlockSpec(memory_space=pl.ANY)] * len(grads)
    return call(
        kernel, "weights_back", at, steps, [*arrays, weight, hidden, both, *grads], in_specs,
        [jax.ShapeDtypeStruct(s, BF16) for s in shapes],
        [
            spec((ck, ff), lambda k, s: (s[0] * steps + k, 0)),
            spec((ck, ff), lambda k, s: (s[0] * steps + k, 0)),
            spec((ff, ck), lambda k, s: (0, s[0] * steps + k)),
        ],
        aliases={n + 4 + i: i for i in range(len(grads))},
        flops=6 * count * width * ff,
    )


def bundle(own, x, y, rows):
    n, width = own.shape
    ck = chunk_of(width, 896)

    def kernel(own_ref, x_ref, y_ref, to_x_ref, to_y_ref):
        for out, more in ((to_x_ref, y_ref), (to_y_ref, x_ref)):
            out[:n, :] = own_ref[...]
            out[n:, :] = more[...]

    out = jax.ShapeDtypeStruct((n + rows, width), own.dtype)
    whole = spec((n + rows, ck), lambda k: (0, k))
    return pl.pallas_call(
        kernel,
        out_shape=[out, out],
        grid=(width // ck,),
        in_specs=[
            spec((n, ck), lambda k: (0, k)),
            spec((rows, ck), lambda k: (0, k)),
            spec((rows, ck), lambda k: (1, k)),
        ],
        out_specs=[whole, whole],
        compiler_params=pltpu.CompilerParams(vmem_limit_bytes=BUNDLE * 2**20),
        cost_estimate=pl.CostEstimate(flops=0, bytes_accessed=4 * out.size * 2, transcendentals=0),
        name="bundle",
    )(own, x, y)


def onward(mine, xs, ys, later):
    _, rows, width = mine.shape
    h, ck = rows // 2, chunk_of(width, 896)

    def kernel(e_ref, n_ref, x_ref, y_ref, *refs):
        to_x_ref, to_y_ref = refs[-2:]
        to_x_ref[:h, :] = e_ref[0, :h, :]
        to_x_ref[h:rows, :] = (e_ref[0, h:, :].astype(F32) + y_ref[...].astype(F32)).astype(BF16)
        to_y_ref[:h, :] = (n_ref[0, :h, :].astype(F32) + x_ref[...].astype(F32)).astype(BF16)
        to_y_ref[h:rows, :] = n_ref[0, h:, :]
        if later is not None:
            to_x_ref[rows:, :] = refs[0][0, :h, :]
            to_y_ref[rows:, :] = refs[0][0, h:, :]

    more = [] if later is None else [later]
    end = xs.shape[0] // h - 1
    out = jax.ShapeDtypeStruct((rows + h * len(more), width), BF16)
    block = lambda i: spec((1, rows, ck), lambda k: (i, 0, k))
    half = spec((h, ck), lambda k: (end, k))
    whole = spec((out.shape[0], ck), lambda k: (0, k))
    return pl.pallas_call(
        kernel,
        out_shape=[out, out],
        grid=(width // ck,),
        in_specs=[block(1), block(2), half, half] + [block(3)] * len(more),
        out_specs=[whole, whole],
        compiler_params=pltpu.CompilerParams(vmem_limit_bytes=BUNDLE * 2**20),
        cost_estimate=pl.CostEstimate(flops=0, bytes_accessed=8 * out.size, transcendentals=0),
        name="onward",
    )(mine, mine, xs, ys, *more)


def gather_both(links, both, table, use):
    X, Y = far_masks()
    shards = lax.axis_size("tensor")
    rows = both.shape[0] // 2
    hop, xs, ys, near = {0: both}, {}, {}, {}
    tables = [table]
    for r in range(shards + 2):
        work = ()
        if r < shards - 1:
            hop[r + 1] = links.send(0, hop[r])
        if r <= shards:
            if r == 0:
                to_x = to_y = both
            elif r < shards:
                to_x, to_y = bundle(hop[r], xs[r - 1], ys[r - 1], rows)
            else:
                to_x, to_y = ys[r - 1][rows : 2 * rows], xs[r - 1][:rows]
            xs[r] = links.send(X, to_x)
            ys[r] = links.send(Y, to_y)
        if r == 0:
            tables += [links.send(X, table), links.send(Y, table)]
        if r == 1:
            tables.append(links.send(Y, tables[1]))
        if r == 2:
            tables += list(links.send(1, jnp.stack(tables)))
        if 1 <= r <= shards + 1:
            arrays = ([hop[r - 1]] if r <= shards else []) + [xs[r - 1], ys[r - 1]]
            near[r - 1] = [links.send(1, a) for a in arrays]
        if 2 <= r:
            q = r - 2
            block = 2 if q + 1 < shards else 0
            pieces = []
            for here, late in (
                ((hop[q], xs[q], ys[q]), (xs[q + 1], ys[q + 1])),
                (near[q], near[q + 1][-2:]),
            ):
                pieces += [(a, 2 * rows, 0) for a in here] + [(a, rows, block) for a in late]
            tok = [(0, 0), (1, 0), (2, 0), (4, 0), (5, 0), (6, 0), (7, 0), (9, 0)]
            grd = [(0, rows), (1, rows), (2, rows), (3, 0), (5, rows), (6, rows), (7, rows), (8, 0)]
            work = use(q, (pieces, tok, grd), tables)
        links.turn(*work)


def gather_plain(own, table, use):
    rows = own.shape[0] // 2
    tables = [table]
    for m in far_masks() + [1]:
        tables = tables + [swap(t, m) for t in tables]
    for j in range(lax.axis_size("tensor")):
        own = ring(own) if j else own
        pieces = [own]
        for m in far_masks() + [1]:
            pieces = pieces + [swap(p, m) for p in pieces]
        places = range(len(pieces))
        pieces = [(a, 2 * rows, 0) for a in pieces]
        use(j, (pieces, [(i, 0) for i in places], [(i, rows) for i in places]), tables)


def plus(*terms):
    return functools.reduce(lambda a, b: a + b, [t.astype(F32) for t in terms]).astype(BF16)


def on_device(tokens, grad_out, expert_ids, gates, w_gate, w_up, w_down):
    owners, shards = lax.axis_size("expert"), lax.axis_size("tensor")
    me, z = lax.axis_index("expert"), lax.axis_index("tensor")
    rows, width = tokens.shape
    wg, wu, wd = w_gate[0], w_up[0], w_down[0]
    far = far_masks()

    chosen = expert_ids[:, :, None] == jnp.arange(owners, dtype=jnp.int32)
    table = jnp.sum(jnp.where(chosen, gates[:, :, None], 0.0), axis=1).T
    at = [lax.rem(z - j + shards, shards).reshape(1) for j in range(shards)]
    both = jnp.concatenate([tokens, grad_out])
    kept, state = [], {"sums": ()}

    def use(j, parts, tables):
        if j == 0:
            w = [lax.dynamic_index_in_dim(t, me, 0, False) for t in tables]
            state["weight"] = jnp.stack(w).reshape(-1, 1)
        kept.append(parts)
        state["sums"] = forward(
            at[j], parts, rows, state["weight"], wg, wu, wd, state["sums"], j == shards - 1
        )
        return state["sums"]

    links = Links(True)
    if len(far) == 2:
        gather_both(links, both, table, use)
    else:
        gather_plain(both, table, use)
    hidden, dboth = state["sums"]

    order = list(range(1, shards)) + [0]
    grads = ()

    def grads_of(i, *first):
        late = [after(a, *first) for a in (hidden, dboth)]
        return weights_back(
            at[i], kept[i], rows, state["weight"], *late, (wg.shape, wu.shape, wd.shape), grads
        )

    def near_of(j, *first):
        late = after(dboth, *first) if first else dboth
        return inputs_back(at[j], late, wg, wu, width, 1)

    mine_of = lambda j, got: inputs_back(at[j], dboth, wg, wu, width, 0, got).reshape(-1, rows, width)
    if len(far) == 2:
        X, Y = far
        links = Links(True)
        n, h = shards, rows // 2
        near, got, mine, acc, hop, xs, ys = {0: near_of(order[0])}, {}, {}, {}, {}, {}, {}
        for r in range(1, n + 3):
            last = list(links.held)
            if 4 <= r:
                q = r - 4
                m = mine[q]
                from_x, from_y = xs[q + 3][:rows], ys[q + 3][:rows]
                acc[q] = plus(m[0], from_x, from_y, *([hop[q - 1]] if q else []))
                hop[q] = links.send(0, acc[q])
            if 2 <= r <= n + 1:
                mine[r - 2] = mine_of(order[r - 2], got[r - 2])
            if 3 <= r:
                to_x, to_y = onward(mine[r - 3], xs[r - 1], ys[r - 1], mine.get(r - 2))
            elif r == 2:
                to_x, to_y = mine[0][3, :h], mine[0][3, h:]
            if 2 <= r:
                xs[r] = links.send(X, to_x)
                ys[r] = links.send(Y, to_y)
            if r <= n:
                got[r - 1] = links.send(1, near[r - 1])
            work = []
            if r < n:
                near[r] = near_of(order[r], *last)
                work.append(near[r])
            if r >= FROM and r - FROM < shards:
                grads = grads_of(r - FROM, *last)
                work = work + list(grads)
            links.turn(*work)
        result = plus(mine[n - 1][0], xs[n + 2][:rows], ys[n + 2][:rows], hop[n - 2])
        for i in range(max(0, n + 3 - FROM), shards):
            grads = grads_of(i)
    else:
        result = None
        for j in order:
            mine = mine_of(j, swap(near_of(j), 1))
            for m in reversed(far):
                cut = mine.shape[0] // 2
                mine = plus(mine[:cut], swap(mine[cut:], m))
            terms = [mine[0]] if result is None else [mine[0], ring(result)]
            result = plus(*terms)
        for j in range(shards):
            grads = grads_of(j)
    return (result, grads[0][None], grads[1][None], grads[2][None])


def solution(mesh):
    placed = (
        P("expert", "tensor"),
        P("expert", "tensor"),
        P("expert", None),
        P("expert", None),
        P("expert", None, "tensor"),
        P("expert", None, "tensor"),
        P("expert", "tensor", None),
    )
    return jax.shard_map(
        on_device,
        mesh=mesh,
        in_specs=placed,
        out_specs=(
            P("expert", "tensor"),
            P("expert", None, "tensor"),
            P("expert", None, "tensor"),
            P("expert", "tensor", None),
        ),
        check_vma=False,
    )
```
